1024 devices in a mesh: table: 64 (over z, core), dp: 16 (over x, y).
Axes of the slice: x: 4, y: 4, z: 32, core: 2. Of those that a mesh axis runs over, the one named last changes fastest.
Arguments:
- emb_table: float32 [3, 16384, 256], P(None, 'table'), may hold values from -4 to 4
- row_request: int32 [64, 16, 3, 64, 8], P('table', 'dp'), may hold values from 0 to 255, as said below
- live_count: int32 [64, 16, 3, 64], P('table', 'dp'), may hold values from 4 to 8, as said below
- inverse: int32 [64, 16, 3, 2048], P('table', 'dp'), may hold values from 0 to 511, as said below
- bag_ids: int32 [64, 16, 3, 2048], P('table', 'dp'), may hold values from 0 to 511, never falling along the last dimension, each value on 1 to 8 neighbouring positions
- labels: int32 [524288], P(('table', 'dp')), may hold values 0 or 1
- w_hidden: bfloat16 [768, 512], replicated, may hold values from -0.21875 to 0.21875
- b_hidden: float32 [512], replicated, may hold values from -3 to 3
- w_out: float32 [512], replicated, may hold values from -0.25 to 0.25
Outputs:
- emb_grad: float32 [16, 3, 16384, 256], P('dp', None, 'table')
- grad_w_hidden: float32 [768, 512], replicated
- grad_b_hidden: float32 [512], replicated
- grad_w_out: float32 [512], replicated
The draws below stay inside these ranges and needn't reach their ends.
Inputs may be any that keep to these rules, and one draw needn't show every extreme that they name: `row_request`: for each device, table and owner the 8 ids are distinct. `live_count`: for each device and table at least one owner has all 8 slots live. `inverse`: every entry p * 8 + c names a live slot: c < live_count of that device, table and owner p.
All inputs are finite; a program needn't handle non-finite values. No bound on the sum of `labels` on one device may be relied on, other than what follows from the above.
Results may differ from the reference program's by a relative error of at most 0.0026.
Values sent between devices are 32-bit elements; how exact they have to be, the bound alone decides.
No kernel may reach another device: no remote copies, remote signals or barrier semaphores. Data moves between devices by JAX's collectives and lax.ppermute only.
A program may use at most 32 MiB of HBM per device.

```python
import math
import jax
import jax.numpy as jnp
import numpy as np
from jax import lax

E = 256
H = 512
TABLES = 3
POOL = 4
ROWS_DEV = 256
CAP = 8
TOK_DEV = 512
SLOTS = 2048
UNIQUE = 512
ROWS = 16384
TOKENS = 524288
N_TABLE = 64
N_DP = 16


def make_counts(key):
    key = jax.random.fold_in(key, 101)
    first, second = jax.random.split(key)
    base = jax.random.randint(first, (N_TABLE, N_DP, TABLES, N_TABLE), CAP // 2, CAP + 1)
    chosen = jax.random.randint(second, (N_TABLE, N_DP, TABLES, 1), 0, N_TABLE)
    owners = jax.lax.broadcasted_iota(jnp.int32, (N_TABLE, N_DP, TABLES, N_TABLE), 3)
    return jnp.where(owners == chosen, CAP, base).astype(jnp.int32)


def draw_live_count(key, part):
    return make_counts(key)


def draw_inverse(key, part):
    counts = make_counts(key)
    key = jax.random.fold_in(key, 7)
    keys = jax.random.split(key, 5)
    shape = (N_TABLE, N_DP, TABLES, SLOTS)
    first = jax.random.randint(keys[0], shape, 0, N_TABLE)
    second = jax.random.randint(keys[1], shape, 0, N_TABLE)
    offset = jax.random.randint(keys[2], (N_TABLE, N_DP, TABLES, 1), 0, N_TABLE)
    owner = (jnp.minimum(first, second) + offset) % N_TABLE
    limit = jnp.take_along_axis(counts, owner, axis=3)
    slot_one = jax.random.randint(keys[3], shape, 0, limit)
    slot_two = jax.random.randint(keys[4], shape, 0, limit)
    return (owner * CAP + jnp.minimum(slot_one, slot_two)).astype(jnp.int32)


def draw_row_request(key, part):
    key = jax.random.fold_in(key, 3)
    first, second = jax.random.split(key)
    shape = (N_TABLE, N_DP, TABLES, N_TABLE, 1)
    base = jax.random.randint(first, shape, 0, ROWS_DEV)
    stride = jax.random.randint(second, shape, 1, ROWS_DEV // CAP + 1)
    offsets = jnp.arange(CAP, dtype=jnp.int32)
    return ((base + offsets * stride) % ROWS_DEV).astype(jnp.int32)


def with_ends(array, own_key, least, high):
    longest = array.shape.index(max(array.shape))
    spots = []
    for shift in (0, 1):
        where = [jax.random.randint(jax.random.fold_in(own_key, axis), (), 0, length) for axis, length in enumerate(array.shape)]
        where[longest] = (where[longest] + shift) % array.shape[longest]
        spots.append(tuple(where))
    return array.at[spots[0]].set(least).at[spots[1]].set(high)


def shard_levels(own_key, dims, shards, least, top_value):
    def one(axis_at, blocks):
        heights = jax.random.uniform(jax.random.fold_in(jax.random.fold_in(own_key, 6), axis_at), (blocks,), jnp.float32, least / len(shards), top_value / len(shards))
        return jnp.repeat(jnp.exp(heights), dims[axis_at] // blocks).reshape((-1,) + (1,) * (len(dims) - axis_at - 1))

    factor_of = one(*shards[0])
    for cut in shards[1:]:
        factor_of = factor_of * one(*cut)
    return factor_of


def split_up(amount, total, bound, slope):
    loads = [(1 << 20) // math.isqrt(grade ** slope) + 1 for grade in range(2, amount + 1)]
    rest, holding = total - bound - (amount - 1), [1] * (amount - 1)
    while rest > 0:
        free = [i for i in range(amount - 1) if holding[i] < bound]
        whole, budget = sum([loads[i] for i in free]), rest
        for i in free:
            addition = min(bound - holding[i], max(1, budget * loads[i] // whole), rest)
            holding[i] = holding[i] + addition
            rest = rest - addition
    return np.array([bound] + holding)


def uneven_parts(stream_key, number_of, total, most, skew):
    if number_of == 2:
        one = jax.random.randint(stream_key, (), max(1, total - most), min(most, total - 1) + 1)
        return jnp.stack([one, total - one])
    lengths = jnp.asarray(split_up(number_of, total, most, skew), jnp.int32)
    couples = (number_of - 1) // 2
    source_of, receiver = lengths[1:1 + 2 * couples:2], lengths[2:2 + 2 * couples:2]
    room = jnp.minimum(source_of - 1, most - receiver)
    passed = jax.random.randint(jax.random.fold_in(stream_key, 1), (couples,), 0, 1 << 20) % (room + 1)
    lengths = lengths.at[1:1 + 2 * couples:2].set(source_of - passed).at[2:2 + 2 * couples:2].set(receiver + passed)
    return lengths[jax.random.permutation(jax.random.fold_in(stream_key, 2), number_of)]


def scatter_about(rng, dims, scale, most, shards=(), held_as=jnp.bfloat16):
    entries = jax.random.normal(rng, dims, jnp.float32) * scale
    if len(shards) > 0:
        entries = shard_levels(rng, dims, shards, -0.22, 0.18) * entries
    return jnp.clip(entries, min=-most, max=most).astype(held_as)


def setup_inputs(seed: int = 0) -> dict:
    arg_keys = jax.random.split(jax.random.key(seed), 10)
    emb_table = scatter_about(arg_keys[0], (TABLES, ROWS, E), 0.5, 4.0, ((1, 64),), jnp.float32)
    row_request = draw_row_request(jax.random.fold_in(arg_keys[9], 71), 0)
    live_count = draw_live_count(jax.random.fold_in(arg_keys[9], 71), 0)
    inverse = draw_inverse(jax.random.fold_in(arg_keys[9], 71), 0)
    bag_ids = jax.vmap(lambda own: jnp.searchsorted(jnp.cumsum(uneven_parts(own, TOK_DEV, SLOTS, 2 * POOL, 2)), jnp.arange(SLOTS), side="right"))(jax.random.split(arg_keys[4], N_TABLE * N_DP * TABLES)).reshape((N_TABLE, N_DP, TABLES, SLOTS)).astype(jnp.int32)
    labels = with_ends((jax.random.randint(arg_keys[5], (TOKENS,), 0, 4) < 1).astype(jnp.int32), jax.random.fold_in(arg_keys[5], 1), 0, 1)
    w_hidden = scatter_about(arg_keys[6], (TABLES * E, H), (TABLES * E) ** -0.5, 0.21875)
    b_hidden = scatter_about(arg_keys[7], (H,), 0.5, 3.0, (), jnp.float32)
    w_out = scatter_about(arg_keys[8], (H,), H ** -0.5, 0.25, (), jnp.float32)
    return {"emb_table": emb_table, "row_request": row_request, "live_count": live_count, "inverse": inverse, "bag_ids": bag_ids, "labels": labels, "w_hidden": w_hidden, "b_hidden": b_hidden, "w_out": w_out}


def pick_rows(table_rows, index):
    return table_rows[index]


def pool_slots(slot_rows, segment):
    return jax.ops.segment_sum(slot_rows, segment, num_segments=TOK_DEV, indices_are_sorted=True)


def gather_back(unique_rows, index):
    return jax.ops.segment_sum(unique_rows, index, num_segments=UNIQUE)


def add_rows(grad_table, index, values):
    return grad_table.at[index.reshape(-1)].add(values.reshape(-1, E))


def device_pass(emb_table, request, count, inverse, bag_ids, label_row, w_hidden, b_hidden, w_out):
    owners = lax.broadcasted_iota(jnp.int32, (TABLES, N_TABLE, CAP), 1)
    global_rows = (request + owners * ROWS_DEV).astype(jnp.int32)
    slot_index = lax.broadcasted_iota(jnp.int32, (TABLES, N_TABLE, CAP), 2)
    live_mask = (slot_index < count[:, :, None]).astype(jnp.float32)
    fetched = jax.vmap(pick_rows)(emb_table, global_rows) * live_mask[..., None]
    unique_rows = fetched.reshape(TABLES, UNIQUE, E)
    slot_rows = jax.vmap(pick_rows)(unique_rows, inverse)
    pooled = jax.vmap(pool_slots)(slot_rows, bag_ids)
    features = jnp.transpose(pooled, (1, 0, 2)).reshape(TOK_DEV, TABLES * E).astype(jnp.bfloat16)
    pre = jnp.dot(features, w_hidden, preferred_element_type=jnp.float32) + b_hidden
    sigma = jax.nn.sigmoid(pre)
    hidden = pre * sigma
    logit = jnp.dot(hidden, w_out, precision=lax.Precision.HIGHEST)
    error = jax.nn.sigmoid(logit) - label_row.astype(jnp.float32)
    grad_pre = error[:, None] * w_out[None, :] * sigma * (1.0 + pre * (1.0 - sigma))
    grad_pre_b = grad_pre.astype(jnp.bfloat16)
    term_w = lax.dot_general(features, grad_pre_b, (((0,), (0,)), ((), ())), preferred_element_type=jnp.float32)
    term_b = jnp.sum(grad_pre, axis=0)
    term_out = jnp.dot(error, hidden, precision=lax.Precision.HIGHEST)
    grad_features = lax.dot_general(grad_pre_b, w_hidden, (((1,), (1,)), ((), ())), preferred_element_type=jnp.float32)
    grad_tables = jnp.transpose(grad_features.reshape(TOK_DEV, TABLES, E), (1, 0, 2))
    slot_grad = jax.vmap(pick_rows)(grad_tables, bag_ids)
    unique_grad = jax.vmap(gather_back)(slot_grad, inverse).reshape(TABLES, N_TABLE, CAP, E)
    return unique_grad, global_rows, term_w, term_b, term_out


def reference(emb_table, row_request, live_count, inverse, bag_ids, labels, w_hidden, b_hidden, w_out):
    label_rows = labels.reshape(N_TABLE, N_DP, TOK_DEV)

    def per_group(sums, group):
        def per_device(carry, member):
            grad_table, sum_w, sum_b, sum_out = carry
            unique_grad, global_rows, term_w, term_b, term_out = device_pass(
                emb_table, row_request[member, group], live_count[member, group], inverse[member, group],
                bag_ids[member, group], label_rows[member, group], w_hidden, b_hidden, w_out)
            grad_table = jax.vmap(add_rows)(grad_table, global_rows, unique_grad)
            return (grad_table, sum_w + term_w, sum_b + term_b, sum_out + term_out), None

        start = (jnp.zeros((TABLES, ROWS, E), jnp.float32),) + sums
        final, unused = lax.scan(per_device, start, jnp.arange(N_TABLE))
        return final[1:], final[0]

    zeros = (jnp.zeros((TABLES * E, H), jnp.float32), jnp.zeros((H,), jnp.float32), jnp.zeros((H,), jnp.float32))
    sums, emb_grad = lax.scan(per_group, zeros, jnp.arange(N_DP))
    return emb_grad, sums[0] / TOKENS, sums[1] / TOKENS, sums[2] / TOKENS
```

```python
import jax
import jax.numpy as jnp
from jax import lax
from jax.experimental import pallas as pl
from jax.experimental.pallas import tpu as pltpu
from jax.sharding import Mesh, PartitionSpec as P

F32 = jnp.float32
BF16 = jnp.bfloat16
LANES = 128
TABLES = 3
ROWS_DEV = 256
WIDTH = 256
CAP = 8
N_FAR = 4
N_MID = 4
N_NEAR = 2
N_CORE = 2
N_DP = 16
N_Z = N_FAR * N_MID * N_NEAR
N_HELD = N_FAR * N_MID
N_TABLE = N_Z * N_CORE
LAYER = N_CORE * N_DP
GROUP = N_NEAR * LAYER
REQUEST_ROWS = 8
SLICE = WIDTH // N_DP
PACK = LANES // SLICE
BLOCKS = N_HELD // PACK
SAMPLES = 512
SLOTS = 2048
UNIQUE = N_TABLE * CAP
HIDDEN = 512
FEATURES = TABLES * WIDTH
TOKENS = SAMPLES * N_TABLE * N_DP
LANE_BLOCKS = HIDDEN // LANES
PIECE = FEATURES // LAYER
PIECE_ROWS = PIECE * LANE_BLOCKS
SUM_ROWS = PIECE_ROWS + 8
FAR = ("far1", "far0")
MID = ("mid1", "mid0")
COLUMN = (*FAR, *MID, "near", "core")
DP = ("x1", "x0", "y1", "y0")
SERVERS = ("near", "core", *DP)
SUMMERS = ("core", "y0", "x0", "y1", "x1")
CHUNK = 32
VMEM = 56 * 1024 * 1024


def params():
    return pltpu.CompilerParams(vmem_limit_bytes=VMEM)


def two_parts(x):
    high = x.astype(BF16)
    return high, (x - high.astype(F32)).astype(BF16)


def dot(a, b, dims=((1,), (0,))):
    return lax.dot_general(a, b, (dims, ((), ())), preferred_element_type=F32)


def slice_kernel(dp_ref, table_ref, request_ref, after_ref, out_ref, turned):
    dp = dp_ref[0]
    half = pl.multiple_of(dp // PACK * LANES, LANES)
    first = pl.multiple_of(dp % PACK * SLICE, SLICE)
    for t in range(TABLES):
        turned[...] = table_ref[t, :, pl.ds(half, LANES)].T
        out_ref[t * SLICE : (t + 1) * SLICE] = turned[pl.ds(first, SLICE), :]
    out_ref[TABLES * SLICE :] = request_ref[...]


def slice_rows(dp, emb_table, requests, after):
    whole = pl.BlockSpec(memory_space=pltpu.VMEM)
    return pl.pallas_call(
        slice_kernel,
        out_shape=jax.ShapeDtypeStruct((TABLES * SLICE + REQUEST_ROWS, ROWS_DEV), F32),
        in_specs=[pl.BlockSpec(memory_space=pltpu.SMEM), whole, whole, pl.BlockSpec(memory_space=pl.ANY)],
        out_specs=whole,
        scratch_shapes=[pltpu.VMEM((LANES, ROWS_DEV), F32)],
        compiler_params=params(),
        name="slice_rows",
    )(dp, emb_table, requests, after)


def serve_kernel(me_ref, ids_ref, slab_ref, out_ref):
    asked = GROUP * CAP
    ids = ids_ref[:, 0].reshape(asked, N_HELD)
    row = lax.broadcasted_iota(jnp.int32, (asked, ROWS_DEV), 1)
    group = lax.broadcasted_iota(jnp.int32, (asked, LANES), 1) // SLICE
    for block in range(BLOCKS):
        slab = slab_ref[block * PACK // N_FAR : (block + 1) * PACK // N_FAR].reshape(LANES, ROWS_DEV).T
        stack = jnp.concatenate(two_parts(slab), axis=1)
        total = jnp.zeros((asked, LANES), F32)
        for owner in range(PACK):
            z = block * PACK + owner
            onehot = jnp.where(ids[:, z : z + 1] == row, 1.0, 0.0).astype(BF16)
            both = dot(onehot, stack)
            total = jnp.where(group == owner, both[:, :LANES] + both[:, LANES:], total)
        for i in range(GROUP):
            out_ref[me_ref[0] ^ i, 0, block] = total[i * CAP : (i + 1) * CAP]


def serve_rows(me, ids, slab):
    return pl.pallas_call(
        serve_kernel,
        grid=(TABLES,),
        out_shape=jax.ShapeDtypeStruct((GROUP, TABLES, BLOCKS, CAP, LANES), F32),
        in_specs=[
            pl.BlockSpec(memory_space=pltpu.SMEM),
            pl.BlockSpec((GROUP, 1, CAP, N_HELD), lambda t: (0, t, 0, 0)),
            pl.BlockSpec((N_MID, N_FAR, SLICE, ROWS_DEV), lambda t: (0, 0, t, 0)),
        ],
        out_specs=pl.BlockSpec((GROUP, 1, BLOCKS, CAP, LANES), lambda t: (0, t, 0, 0, 0)),
        compiler_params=params(),
        name="serve_rows",
    )(me, ids, slab)


def count_kernel(inverse_ref, bag_ref, live_ref, count_ref, turned_ref):
    sample = lax.broadcasted_iota(jnp.int32, (SAMPLES, SLOTS), 0)
    unique = lax.broadcasted_iota(jnp.int32, (UNIQUE, SLOTS), 0)
    in_bag = jnp.where(sample == bag_ref[0], 1.0, 0.0).astype(BF16)
    in_slot = jnp.where(unique == inverse_ref[0], 1.0, 0.0).astype(BF16)
    counts = dot(in_bag, in_slot, ((1,), (1,)))
    count_ref[0] = (counts * live_ref[0]).astype(BF16)
    turned_ref[0] = counts.T.astype(BF16)


def count_slots(inverse, bag_ids, live):
    row = lambda t: (t, 0, 0)
    return pl.pallas_call(
        count_kernel,
        grid=(TABLES,),
        out_shape=[
            jax.ShapeDtypeStruct((TABLES, SAMPLES, UNIQUE), BF16),
            jax.ShapeDtypeStruct((TABLES, UNIQUE, SAMPLES), BF16),
        ],
        in_specs=[
            pl.BlockSpec((1, 1, SLOTS), row),
            pl.BlockSpec((1, 1, SLOTS), row),
            pl.BlockSpec((1, 1, UNIQUE), row),
        ],
        out_specs=[
            pl.BlockSpec((1, SAMPLES, UNIQUE), row),
            pl.BlockSpec((1, UNIQUE, SAMPLES), row),
        ],
        compiler_params=params(),
        name="count_slots",
    )(inverse, bag_ids, live)


def exchange_groups(tiles):
    group = lax.broadcasted_iota(jnp.int32, tiles[0].shape, 1) // SLICE
    step = PACK // 2
    while step:
        low_half = (group & step) == 0
        swapped = list(tiles)
        for i in range(PACK):
            if i & step == 0:
                a, b = tiles[i], tiles[i + step]
                swapped[i] = jnp.where(low_half, a, pltpu.roll(b, step * SLICE, 1))
                swapped[i + step] = jnp.where(low_half, pltpu.roll(a, LANES - step * SLICE, 1), b)
        tiles = swapped
        step //= 2
    return tiles


def tower_kernel(fetched_ref, count_ref, turned_ref, w_hidden_ref, bias_ref, w_out_ref, label_ref,
                 back_ref, feature_ref, grad_pre_ref, extra_ref, unique, pre):
    for t in range(TABLES):
        for source in range(N_NEAR * N_CORE):
            for half in range(N_DP // PACK):
                first = source * N_DP + half * PACK
                tiles = [fetched_ref[first + i, t].reshape(BLOCKS * CAP, LANES) for i in range(PACK)]
                for owner, tile in enumerate(exchange_groups(tiles)):
                    held = tile.reshape(BLOCKS, CAP, LANES)
                    for block in range(BLOCKS):
                        mid, far = divmod(block * PACK + owner, N_FAR)
                        unique[far, mid, source, :, half * LANES : (half + 1) * LANES] = held[block]
        high, low = two_parts(unique[...].reshape(UNIQUE, WIDTH))
        counts = count_ref[t]
        pooled = dot(counts, high) + dot(counts, low)
        feature_ref[:, t * WIDTH : (t + 1) * WIDTH] = pooled.astype(BF16)
    pre[...] = dot(feature_ref[...], w_hidden_ref[...]) + bias_ref[...]

    def chunk(i, sums):
        rows = pl.ds(pl.multiple_of(i * CHUNK, CHUNK), CHUNK)
        w_out = w_out_ref[...]
        x = pre[rows, :]
        sigma = jax.nn.sigmoid(x)
        hidden = x * sigma
        logit = jnp.sum(hidden * w_out, axis=1, keepdims=True)
        error = jax.nn.sigmoid(logit) - label_ref[rows, :].astype(F32)
        grad_pre = error * w_out * sigma * (1.0 + x * (1.0 - sigma))
        grad_pre_ref[rows, :] = grad_pre.astype(BF16)
        fold = lambda v: jnp.sum(v.reshape(CHUNK // 8, 8, HIDDEN), axis=0)
        return sums[0] + fold(grad_pre), sums[1] + fold(error * hidden)

    start = jnp.zeros((8, HIDDEN), F32)
    sums = lax.fori_loop(0, SAMPLES // CHUNK, chunk, (start, start))
    for which in range(2):
        row = jnp.sum(sums[which], axis=0, keepdims=True)
        for block in range(LANE_BLOCKS):
            at = which * LANE_BLOCKS + block
            extra_ref[at : at + 1, :] = row[:, block * LANES : (block + 1) * LANES]
    grad_pre = grad_pre_ref[...]
    for t in range(TABLES):
        grad = dot(grad_pre, w_hidden_ref[t * WIDTH : (t + 1) * WIDTH, :], ((1,), (1,)))
        high, low = two_parts(grad)
        turned = turned_ref[t]
        back_ref[:, t] = (dot(turned, high) + dot(turned, low)).reshape(N_TABLE, CAP, WIDTH)


def tower(fetched, counts, turned, w_hidden, b_hidden, w_out, labels):
    whole = pl.BlockSpec(memory_space=pltpu.VMEM)
    return pl.pallas_call(
        tower_kernel,
        out_shape=[
            jax.ShapeDtypeStruct((N_TABLE, TABLES, CAP, WIDTH), F32),
            jax.ShapeDtypeStruct((SAMPLES, FEATURES), BF16),
            jax.ShapeDtypeStruct((SAMPLES, HIDDEN), BF16),
            jax.ShapeDtypeStruct((8, LANES), F32),
        ],
        in_specs=[whole] * 7,
        out_specs=[whole] * 4,
        scratch_shapes=[
            pltpu.VMEM((N_FAR, N_MID, N_NEAR * N_CORE, CAP, WIDTH), F32),
            pltpu.VMEM((SAMPLES, HIDDEN), F32),
        ],
        compiler_params=params(),
        name="tower",
    )(fetched, counts, turned, w_hidden, b_hidden, w_out, labels)


def piece_rows(piece):
    return pl.ds(pl.multiple_of(piece * PIECE, 8), PIECE)


def lanes(block):
    return pl.ds(block * LANES, LANES)


def weight_kernel(me_ref, feature_ref, grad_pre_ref, extra_ref, out_ref, grad):
    grad[...] = dot(feature_ref[...], grad_pre_ref[...], ((0,), (0,)))
    for i in range(LAYER):
        for block in range(LANE_BLOCKS):
            out_ref[i, block * PIECE : (block + 1) * PIECE, :] = grad[piece_rows(me_ref[0] ^ i), lanes(block)]
        out_ref[i, PIECE_ROWS:, :] = extra_ref[...]


def weight_pieces(me, features, grad_pre, extra):
    whole = pl.BlockSpec(memory_space=pltpu.VMEM)
    return pl.pallas_call(
        weight_kernel,
        out_shape=jax.ShapeDtypeStruct((LAYER, SUM_ROWS, LANES), F32),
        in_specs=[pl.BlockSpec(memory_space=pltpu.SMEM)] + [whole] * 3,
        out_specs=whole,
        scratch_shapes=[pltpu.VMEM((FEATURES, HIDDEN), F32)],
        compiler_params=params(),
        name="weight_pieces",
    )(me, features, grad_pre, extra)


def unpack_kernel(me_ref, low_ref, high_ref, w_hidden_ref, bias_ref, w_out_ref):
    for i in range(LAYER):
        piece_ref = high_ref if i >= LAYER // 2 else low_ref
        for block in range(LANE_BLOCKS):
            w_hidden_ref[piece_rows(me_ref[0] ^ i), lanes(block)] = (
                piece_ref[i % (LAYER // 2), block * PIECE : (block + 1) * PIECE, :] / TOKENS
            )
    for block in range(LANE_BLOCKS):
        at = PIECE_ROWS + block
        bias_ref[:, lanes(block)] = low_ref[0, at : at + 1, :] / TOKENS
        at = at + LANE_BLOCKS
        w_out_ref[:, lanes(block)] = low_ref[0, at : at + 1, :] / TOKENS


def unpack(me, low, high):
    whole = pl.BlockSpec(memory_space=pltpu.VMEM)
    return pl.pallas_call(
        unpack_kernel,
        out_shape=[
            jax.ShapeDtypeStruct((FEATURES, HIDDEN), F32),
            jax.ShapeDtypeStruct((1, HIDDEN), F32),
            jax.ShapeDtypeStruct((1, HIDDEN), F32),
        ],
        in_specs=[pl.BlockSpec(memory_space=pltpu.SMEM)] + [whole] * 2,
        out_specs=[whole] * 3,
        compiler_params=params(),
        name="unpack",
    )(me, low, high)


def scatter_kernel(ids_ref, returned_ref, out_ref):
    row = lax.broadcasted_iota(jnp.int32, (ROWS_DEV, UNIQUE), 0)
    onehot = jnp.where(row == ids_ref[0], 1.0, 0.0).astype(BF16)
    high, low = two_parts(returned_ref[:, 0].reshape(UNIQUE, WIDTH))
    out_ref[0] = dot(onehot, high) + dot(onehot, low)


def scatter_rows(ids, returned):
    return pl.pallas_call(
        scatter_kernel,
        grid=(TABLES,),
        out_shape=jax.ShapeDtypeStruct((TABLES, ROWS_DEV, WIDTH), F32),
        in_specs=[
            pl.BlockSpec((1, 1, UNIQUE), lambda t: (t, 0, 0)),
            pl.BlockSpec((N_TABLE, 1, CAP, WIDTH), lambda t: (0, t, 0, 0)),
        ],
        out_specs=pl.BlockSpec((1, ROWS_DEV, WIDTH), lambda t: (t, 0, 0)),
        compiler_params=params(),
        name="scatter_rows",
    )(ids, returned)


def place(axes):
    return lax.axis_index(axes)


def swap(x, axes):
    return lax.all_to_all(x, axes, split_axis=0, concat_axis=0, tiled=True)


def spread(x, axes, count):
    return swap(jnp.broadcast_to(x[None], (count, *x.shape)), axes)


def partner(x, axis):
    return lax.ppermute(x, axis, [(0, 1), (1, 0)])


def pair_swap(x, axes):
    half = x.shape[0] // 2
    for axis in axes:
        x = jnp.stack([x[:half], partner(x[half:], axis)], axis=1).reshape(x.shape)
    return x


def pair_gather(x, axes):
    x = x[None]
    for axis in reversed(axes):
        x = jnp.concatenate([x, partner(x, axis)])
    return x


def relative(x, axes):
    shape = x.shape
    for at, axis in enumerate(axes):
        x = x.reshape(2**at, 2, -1, *shape[1:])
        x = jnp.where(lax.axis_index(axis) == 1, x[:, ::-1], x)
    return x.reshape(shape)


def pair_scatter_sum(x, axes):
    for axis in axes:
        half = x.shape[0] // 2
        x = x[:half] + partner(x[half:], axis)
    return x[0]


def quad_sum(x, axes):
    terms = [x] + [lax.ppermute(x, axes, [(i, i ^ k) for i in range(4)]) for k in range(1, 4)]
    return (terms[0] + terms[1]) + (terms[2] + terms[3])


def shards(emb_table, row_request, live_count, inverse, bag_ids, labels, w_hidden, b_hidden, w_out):
    request = row_request[0, 0]

    near = N_NEAR * N_CORE
    grouped = jnp.transpose(request.reshape(TABLES, N_FAR, N_MID, near, CAP), (3, 0, 4, 2, 1))
    grouped = relative(grouped.reshape(near, TABLES, CAP * N_HELD), ("near", "core"))
    grouped = pair_swap(grouped, ("near",))
    chip = grouped
    grouped = pair_swap(grouped, ("core",))
    ids = jnp.swapaxes(pair_gather(grouped, DP), 0, 1).reshape(GROUP, TABLES, CAP, N_HELD)

    every = jnp.transpose(request, (1, 0, 2)).reshape(N_TABLE, TABLES * CAP).astype(F32)
    every = jnp.pad(every, ((0, 0), (0, LANES // near - TABLES * CAP))).reshape(REQUEST_ROWS, WIDTH)
    slab = spread(slice_rows(place(DP).reshape(1), emb_table, every, chip), FAR, N_FAR)
    slab, ids = lax.optimization_barrier((slab, ids))
    slab = spread(slab, MID, N_MID)

    asked = slab[:, :, TABLES * SLICE :].reshape(N_HELD, REQUEST_ROWS, WIDTH)
    spot = place((*FAR, *MID))
    asked = lax.dynamic_slice(asked, (0, spot // 2, spot % 2 * LANES), (N_HELD, 1, LANES))
    asked = jnp.swapaxes(asked.reshape(N_HELD, near, LANES // near), 0, 1).astype(jnp.int32)
    asked = relative(pair_swap(relative(asked, ("near", "core")), ("near", "core")), ("near", "core"))
    asked = asked[:, :, : TABLES * CAP].reshape(near, N_MID, N_FAR, TABLES, CAP)
    asked = jnp.transpose(asked, (3, 2, 1, 0, 4)).reshape(TABLES, 1, UNIQUE)

    slot = lax.broadcasted_iota(jnp.int32, (TABLES, N_TABLE, CAP), 2)
    live = (slot < live_count[0, 0][:, :, None]).astype(F32).reshape(TABLES, 1, UNIQUE)
    counts, turned = count_slots(
        inverse[0, 0].reshape(TABLES, 1, SLOTS), bag_ids[0, 0].reshape(TABLES, 1, SLOTS), live
    )

    fetched = swap(serve_rows(place(SERVERS).reshape(1), ids, slab), SERVERS)
    fetched, asked = lax.optimization_barrier((fetched, asked))
    back, features, grad_pre, extra = tower(
        fetched,
        counts,
        turned,
        w_hidden,
        b_hidden.reshape(1, HIDDEN),
        w_out.reshape(1, HIDDEN),
        labels.reshape(SAMPLES, 1),
    )
    returned = swap(back, COLUMN)
    grad_shard = scatter_rows(asked, returned)

    me = place(SUMMERS).reshape(1)
    piece = pair_scatter_sum(weight_pieces(me, features, grad_pre, extra), SUMMERS)
    piece = piece + partner(piece, "near")
    piece = quad_sum(quad_sum(piece, MID), FAR)
    low = pair_gather(piece, SUMMERS[1:])
    grad_w, grad_b, grad_out = unpack(me, low, partner(low, SUMMERS[0]))
    return grad_shard[None], grad_w, grad_b.reshape(HIDDEN), grad_out.reshape(HIDDEN)


def solution(mesh):
    split = Mesh(mesh.devices.reshape((2,) * 10), (*COLUMN, *DP))
    return jax.shard_map(
        shards,
        mesh=split,
        in_specs=(
            P(None, COLUMN, None),
            P(COLUMN, DP, None, None, None),
            P(COLUMN, DP, None, None),
            P(COLUMN, DP, None, None),
            P(COLUMN, DP, None, None),
            P((*COLUMN, *DP)),
            P(),
            P(),
            P(),
        ),
        out_specs=(P(DP, None, COLUMN, None), P(), P(), P()),
        check_vma=False,
    )
```

```python
import jax
import jax.numpy as jnp
from jax import lax
from jax.experimental import pallas as pl
from jax.experimental.pallas import tpu as pltpu
from jax.sharding import Mesh, PartitionSpec as P

F32 = jnp.float32
BF16 = jnp.bfloat16
LANES = 128
TABLES = 3
ROWS_DEV = 256
WIDTH = 256
CAP = 8
N_FAR = 4
N_MID = 4
N_NEAR = 2
N_CORE = 2
N_DP = 16
N_Z = N_FAR * N_MID * N_NEAR
N_HELD = N_FAR * N_MID
N_TABLE = N_Z * N_CORE
LAYER = N_CORE * N_DP
GROUP = N_NEAR * LAYER
REQUEST_ROWS = 8
SLICE = WIDTH // N_DP
PACK = LANES // SLICE
BLOCKS = N_HELD // PACK
SAMPLES = 512
SLOTS = 2048
UNIQUE = N_TABLE * CAP
HIDDEN = 512
FEATURES = TABLES * WIDTH
TOKENS = SAMPLES * N_TABLE * N_DP
LANE_BLOCKS = HIDDEN // LANES
PIECE = FEATURES // (GROUP // 2)
HALF_BLOCKS = LANE_BLOCKS // 2
PIECE_ROWS = PIECE * HALF_BLOCKS
SUM_ROWS = PIECE_ROWS + 8
FAR = ("far1", "far0")
MID = ("mid1", "mid0")
COLUMN = (*FAR, *MID, "near", "core")
DP = ("x1", "x0", "y1", "y0")
SERVERS = ("near", "core", *DP)
SUMMERS = ("core", "y0", "x0", "y1", "x1", "near")
CHUNK = 32
VMEM = 56 * 1024 * 1024


def params():
    return pltpu.CompilerParams(vmem_limit_bytes=VMEM)


def two_parts(x):
    high = x.astype(BF16)
    return high, (x - high.astype(F32)).astype(BF16)


def dot(a, b, dims=((1,), (0,))):
    return lax.dot_general(a, b, (dims, ((), ())), preferred_element_type=F32)


def slice_kernel(dp_ref, table_ref, request_ref, out_ref, turned):
    dp = dp_ref[0]
    half = pl.multiple_of(dp // PACK * LANES, LANES)
    first = pl.multiple_of(dp % PACK * SLICE, SLICE)
    for t in range(TABLES):
        turned[...] = table_ref[t, :, pl.ds(half, LANES)].T
        out_ref[t * SLICE : (t + 1) * SLICE] = turned[pl.ds(first, SLICE), :]
    out_ref[TABLES * SLICE :, :LANES] = request_ref[:REQUEST_ROWS]
    out_ref[TABLES * SLICE :, LANES:] = request_ref[REQUEST_ROWS:]


def slice_rows(dp, emb_table, requests):
    whole = pl.BlockSpec(memory_space=pltpu.VMEM)
    return pl.pallas_call(
        slice_kernel,
        out_shape=jax.ShapeDtypeStruct((TABLES * SLICE + REQUEST_ROWS, ROWS_DEV), F32),
        in_specs=[pl.BlockSpec(memory_space=pltpu.SMEM), whole, whole],
        out_specs=whole,
        scratch_shapes=[pltpu.VMEM((LANES, ROWS_DEV), F32)],
        compiler_params=params(),
        name="slice_rows",
    )(dp, emb_table, requests)


def serve_kernel(me_ref, mid_ref, ids_ref, slab_ref, out_ref):
    asked = GROUP * CAP
    ids = ids_ref[:, 0].reshape(asked, N_HELD)
    row = lax.broadcasted_iota(jnp.int32, (asked, ROWS_DEV), 1)
    group = lax.broadcasted_iota(jnp.int32, (asked, LANES), 1) // SLICE
    for block in range(BLOCKS):
        mids = range(block * PACK // N_FAR, (block + 1) * PACK // N_FAR)
        slab = [slab_ref[(mid + N_MID - mid_ref[0]) % N_MID].reshape(N_FAR * SLICE, ROWS_DEV) for mid in mids]
        slab = jnp.concatenate(slab).T
        stack = jnp.concatenate(two_parts(slab), axis=1)
        total = jnp.zeros((asked, LANES), F32)
        for owner in range(PACK):
            z = block * PACK + owner
            onehot = jnp.where(ids[:, z : z + 1] == row, 1.0, 0.0).astype(BF16)
            both = dot(onehot, stack)
            total = jnp.where(group == owner, both[:, :LANES] + both[:, LANES:], total)
        for i in range(GROUP):
            out_ref[me_ref[0] ^ i, 0, block] = total[i * CAP : (i + 1) * CAP]


def serve_rows(me, mid, ids, slab):
    return pl.pallas_call(
        serve_kernel,
        grid=(TABLES,),
        out_shape=jax.ShapeDtypeStruct((GROUP, TABLES, BLOCKS, CAP, LANES), F32),
        in_specs=[
            pl.BlockSpec(memory_space=pltpu.SMEM),
            pl.BlockSpec(memory_space=pltpu.SMEM),
            pl.BlockSpec((GROUP, 1, CAP, N_HELD), lambda t: (0, t, 0, 0)),
            pl.BlockSpec((N_MID, N_FAR, SLICE, ROWS_DEV), lambda t: (0, 0, t, 0)),
        ],
        out_specs=pl.BlockSpec((GROUP, 1, BLOCKS, CAP, LANES), lambda t: (0, t, 0, 0, 0)),
        compiler_params=params(),
        name="serve_rows",
    )(me, mid, ids, slab)


def count_kernel(inverse_ref, bag_ref, live_ref, count_ref, turned_ref):
    sample = lax.broadcasted_iota(jnp.int32, (SAMPLES, SLOTS), 0)
    unique = lax.broadcasted_iota(jnp.int32, (UNIQUE, SLOTS), 0)
    in_bag = jnp.where(sample == bag_ref[0], 1.0, 0.0).astype(BF16)
    in_slot = jnp.where(unique == inverse_ref[0], 1.0, 0.0).astype(BF16)
    counts = dot(in_bag, in_slot, ((1,), (1,)))
    count_ref[0] = (counts * live_ref[0]).astype(BF16)
    turned_ref[0] = counts.T.astype(BF16)


def count_slots(inverse, bag_ids, live):
    row = lambda t: (t, 0, 0)
    return pl.pallas_call(
        count_kernel,
        grid=(TABLES,),
        out_shape=[
            jax.ShapeDtypeStruct((TABLES, SAMPLES, UNIQUE), BF16),
            jax.ShapeDtypeStruct((TABLES, UNIQUE, SAMPLES), BF16),
        ],
        in_specs=[
            pl.BlockSpec((1, 1, SLOTS), row),
            pl.BlockSpec((1, 1, SLOTS), row),
            pl.BlockSpec((1, 1, UNIQUE), row),
        ],
        out_specs=[
            pl.BlockSpec((1, SAMPLES, UNIQUE), row),
            pl.BlockSpec((1, UNIQUE, SAMPLES), row),
        ],
        compiler_params=params(),
        name="count_slots",
    )(inverse, bag_ids, live)


def exchange_groups(tiles):
    group = lax.broadcasted_iota(jnp.int32, tiles[0].shape, 1) // SLICE
    step = PACK // 2
    while step:
        low_half = (group & step) == 0
        swapped = list(tiles)
        for i in range(PACK):
            if i & step == 0:
                a, b = tiles[i], tiles[i + step]
                swapped[i] = jnp.where(low_half, a, pltpu.roll(b, step * SLICE, 1))
                swapped[i + step] = jnp.where(low_half, pltpu.roll(a, LANES - step * SLICE, 1), b)
        tiles = swapped
        step //= 2
    return tiles


def tower_kernel(fetched_ref, count_ref, turned_ref, w_hidden_ref, bias_ref, w_out_ref, label_ref,
                 back_ref, feature_ref, grad_pre_ref, extra_ref, unique, pre):
    for t in range(TABLES):
        for source in range(N_NEAR * N_CORE):
            for half in range(N_DP // PACK):
                first = source * N_DP + half * PACK
                tiles = [fetched_ref[first + i, t].reshape(BLOCKS * CAP, LANES) for i in range(PACK)]
                for owner, tile in enumerate(exchange_groups(tiles)):
                    held = tile.reshape(BLOCKS, CAP, LANES)
                    for block in range(BLOCKS):
                        mid, far = divmod(block * PACK + owner, N_FAR)
                        unique[far, mid, source, :, half * LANES : (half + 1) * LANES] = held[block]
        high, low = two_parts(unique[...].reshape(UNIQUE, WIDTH))
        counts = count_ref[t]
        pooled = dot(counts, high) + dot(counts, low)
        feature_ref[:, t * WIDTH : (t + 1) * WIDTH] = pooled.astype(BF16)
    pre[...] = dot(feature_ref[...], w_hidden_ref[...]) + bias_ref[...]

    def chunk(i, sums):
        rows = pl.ds(pl.multiple_of(i * CHUNK, CHUNK), CHUNK)
        w_out = w_out_ref[...]
        x = pre[rows, :]
        sigma = jax.nn.sigmoid(x)
        hidden = x * sigma
        logit = jnp.sum(hidden * w_out, axis=1, keepdims=True)
        error = jax.nn.sigmoid(logit) - label_ref[rows, :].astype(F32)
        grad_pre = error * w_out * sigma * (1.0 + x * (1.0 - sigma))
        grad_pre_ref[rows, :] = grad_pre.astype(BF16)
        fold = lambda v: jnp.sum(v.reshape(CHUNK // 8, 8, HIDDEN), axis=0)
        return sums[0] + fold(grad_pre), sums[1] + fold(error * hidden)

    start = jnp.zeros((8, HIDDEN), F32)
    sums = lax.fori_loop(0, SAMPLES // CHUNK, chunk, (start, start))
    for which in range(2):
        row = jnp.sum(sums[which], axis=0, keepdims=True)
        for block in range(LANE_BLOCKS):
            at = which * LANE_BLOCKS + block
            extra_ref[at : at + 1, :] = row[:, block * LANES : (block + 1) * LANES]
    grad_pre = grad_pre_ref[...]
    for t in range(TABLES):
        grad = dot(grad_pre, w_hidden_ref[t * WIDTH : (t + 1) * WIDTH, :], ((1,), (1,)))
        high, low = two_parts(grad)
        turned = turned_ref[t]
        back_ref[:, t] = (dot(turned, high) + dot(turned, low)).reshape(N_TABLE, CAP, WIDTH)


def tower(fetched, counts, turned, w_hidden, b_hidden, w_out, labels):
    whole = pl.BlockSpec(memory_space=pltpu.VMEM)
    return pl.pallas_call(
        tower_kernel,
        out_shape=[
            jax.ShapeDtypeStruct((N_TABLE, TABLES, CAP, WIDTH), F32),
            jax.ShapeDtypeStruct((SAMPLES, FEATURES), BF16),
            jax.ShapeDtypeStruct((SAMPLES, HIDDEN), BF16),
            jax.ShapeDtypeStruct((8, LANES), F32),
        ],
        in_specs=[whole] * 7,
        out_specs=[whole] * 4,
        scratch_shapes=[
            pltpu.VMEM((N_FAR, N_MID, N_NEAR * N_CORE, CAP, WIDTH), F32),
            pltpu.VMEM((SAMPLES, HIDDEN), F32),
        ],
        compiler_params=params(),
        name="tower",
    )(fetched, counts, turned, w_hidden, b_hidden, w_out, labels)


def piece_at(piece, block):
    rows = pl.ds(pl.multiple_of((piece >> 1) * PIECE, 8), PIECE)
    columns = pl.ds(pl.multiple_of(((piece & 1) * HALF_BLOCKS + block) * LANES, LANES), LANES)
    return rows, columns


def weight_kernel(me_ref, feature_ref, grad_pre_ref, extra_ref, out_ref, grad):
    grad[...] = dot(feature_ref[...], grad_pre_ref[...], ((0,), (0,)))
    for i in range(GROUP):
        for block in range(HALF_BLOCKS):
            rows, columns = piece_at(me_ref[0] ^ i, block)
            out_ref[i, block * PIECE : (block + 1) * PIECE, :] = grad[rows, columns]
        out_ref[i, PIECE_ROWS:, :] = extra_ref[...]


def weight_pieces(me, features, grad_pre, extra):
    whole = pl.BlockSpec(memory_space=pltpu.VMEM)
    return pl.pallas_call(
        weight_kernel,
        out_shape=jax.ShapeDtypeStruct((GROUP, SUM_ROWS, LANES), F32),
        in_specs=[pl.BlockSpec(memory_space=pltpu.SMEM)] + [whole] * 3,
        out_specs=whole,
        scratch_shapes=[pltpu.VMEM((FEATURES, HIDDEN), F32)],
        compiler_params=params(),
        name="weight_pieces",
    )(me, features, grad_pre, extra)


def unpack_kernel(me_ref, low_ref, high_ref, w_hidden_ref, bias_ref, w_out_ref):
    for i in range(GROUP):
        piece_ref = high_ref if i >= GROUP // 2 else low_ref
        for block in range(HALF_BLOCKS):
            rows, columns = piece_at(me_ref[0] ^ i, block)
            w_hidden_ref[rows, columns] = (
                piece_ref[i % (GROUP // 2), block * PIECE : (block + 1) * PIECE, :] / TOKENS
            )
    for block in range(LANE_BLOCKS):
        at = PIECE_ROWS + block
        columns = pl.ds(block * LANES, LANES)
        bias_ref[:, columns] = low_ref[0, at : at + 1, :] / TOKENS
        at = at + LANE_BLOCKS
        w_out_ref[:, columns] = low_ref[0, at : at + 1, :] / TOKENS


def unpack(me, low, high):
    whole = pl.BlockSpec(memory_space=pltpu.VMEM)
    return pl.pallas_call(
        unpack_kernel,
        out_shape=[
            jax.ShapeDtypeStruct((FEATURES, HIDDEN), F32),
            jax.ShapeDtypeStruct((1, HIDDEN), F32),
            jax.ShapeDtypeStruct((1, HIDDEN), F32),
        ],
        in_specs=[pl.BlockSpec(memory_space=pltpu.SMEM)] + [whole] * 2,
        out_specs=[whole] * 3,
        compiler_params=params(),
        name="unpack",
    )(me, low, high)


def scatter_kernel(ids_ref, returned_ref, out_ref):
    row = lax.broadcasted_iota(jnp.int32, (ROWS_DEV, UNIQUE), 0)
    onehot = jnp.where(row == ids_ref[0], 1.0, 0.0).astype(BF16)
    high, low = two_parts(returned_ref[:, 0].reshape(UNIQUE, WIDTH))
    out_ref[0] = dot(onehot, high) + dot(onehot, low)


def scatter_rows(ids, returned):
    return pl.pallas_call(
        scatter_kernel,
        grid=(TABLES,),
        out_shape=jax.ShapeDtypeStruct((TABLES, ROWS_DEV, WIDTH), F32),
        in_specs=[
            pl.BlockSpec((1, 1, UNIQUE), lambda t: (t, 0, 0)),
            pl.BlockSpec((N_TABLE, 1, CAP, WIDTH), lambda t: (0, t, 0, 0)),
        ],
        out_specs=pl.BlockSpec((1, ROWS_DEV, WIDTH), lambda t: (t, 0, 0)),
        compiler_params=params(),
        name="scatter_rows",
    )(ids, returned)


def place(axes):
    return lax.axis_index(axes)


def swap(x, axes):
    return lax.all_to_all(x, axes, split_axis=0, concat_axis=0, tiled=True)


def spread(x, axes, count):
    return swap(jnp.broadcast_to(x[None], (count, *x.shape)), axes)


def partner(x, axis):
    return lax.ppermute(x, axis, [(0, 1), (1, 0)])


def pair_swap(x, axes):
    half = x.shape[0] // 2
    for axis in axes:
        x = jnp.stack([x[:half], partner(x[half:], axis)], axis=1).reshape(x.shape)
    return x


def pair_gather(x, axes):
    x = x[None]
    for axis in reversed(axes):
        x = jnp.concatenate([x, partner(x, axis)])
    return x


def relative(x, axes):
    shape = x.shape
    for at, axis in enumerate(axes):
        x = x.reshape(2**at, 2, -1, *shape[1:])
        x = jnp.where(lax.axis_index(axis) == 1, x[:, ::-1], x)
    return x.reshape(shape)


def pair_scatter_sum(x, axes):
    for axis in axes:
        half = x.shape[0] // 2
        x = x[:half] + partner(x[half:], axis)
    return x[0]


def shift(x, axes, count, by):
    return lax.ppermute(x, axes, [(i, (i + by) % count) for i in range(count)])


def sum_over_z(x):
    for axis in reversed(MID):
        x = x + partner(x, axis)
    x = x + partner(x, FAR[1])
    return x + lax.ppermute(x, FAR, [(i, N_FAR - 1 - i) for i in range(N_FAR)])


def shards(emb_table, row_request, live_count, inverse, bag_ids, labels, w_hidden, b_hidden, w_out):
    request = row_request[0, 0]

    near = N_NEAR * N_CORE
    grouped = jnp.transpose(request.reshape(TABLES, N_FAR, N_MID, near, CAP), (3, 0, 4, 2, 1))
    grouped = relative(grouped.reshape(near, TABLES, CAP * N_HELD), ("near", "core"))
    grouped = pair_swap(grouped, ("near", "core"))
    ids = jnp.swapaxes(pair_gather(grouped, DP), 0, 1).reshape(GROUP, TABLES, CAP, N_HELD)

    travel = grouped.reshape(near * TABLES, CAP * N_HELD).astype(F32)
    travel = jnp.pad(travel, ((0, 2 * REQUEST_ROWS - near * TABLES), (0, 0)))
    slab = spread(slice_rows(place(DP).reshape(1), emb_table, travel), FAR, N_FAR)
    slab, ids = lax.optimization_barrier((slab, ids))
    held = (*FAR, *MID)
    across = [shift(slab[: N_FAR // 2], held, N_HELD, -2), shift(slab[N_FAR // 2 :], held, N_HELD, 2)]
    slab = jnp.stack([slab, shift(slab, held, N_HELD, -1), jnp.concatenate(across), shift(slab, held, N_HELD, 1)])

    mid = place(MID)
    asked = slab[:, :, TABLES * SLICE :]
    asked = jnp.concatenate([asked[..., :LANES], asked[..., LANES:]], axis=2)[:, :, : near * TABLES]
    asked = asked.reshape(N_MID, N_FAR, near, TABLES, CAP, N_HELD)
    asked = lax.dynamic_index_in_dim(asked, mid * N_FAR + place(FAR), 5, keepdims=False).astype(jnp.int32)
    asked = lax.dynamic_slice_in_dim(jnp.concatenate([asked, asked]), (N_MID - mid) % N_MID, N_MID, axis=0)
    asked = relative(jnp.moveaxis(asked, 2, 0), ("near", "core"))
    asked = jnp.transpose(asked, (3, 2, 1, 0, 4)).reshape(TABLES, 1, UNIQUE)

    slot = lax.broadcasted_iota(jnp.int32, (TABLES, N_TABLE, CAP), 2)
    live = (slot < live_count[0, 0][:, :, None]).astype(F32).reshape(TABLES, 1, UNIQUE)
    counts, turned = count_slots(
        inverse[0, 0].reshape(TABLES, 1, SLOTS), bag_ids[0, 0].reshape(TABLES, 1, SLOTS), live
    )

    slab, counts, turned = lax.optimization_barrier((slab, counts, turned))
    fetched = swap(serve_rows(place(SERVERS).reshape(1), mid.reshape(1), ids, slab), SERVERS)
    fetched, asked = lax.optimization_barrier((fetched, asked))
    back, features, grad_pre, extra = tower(
        fetched,
        counts,
        turned,
        w_hidden,
        b_hidden.reshape(1, HIDDEN),
        w_out.reshape(1, HIDDEN),
        labels.reshape(SAMPLES, 1),
    )
    returned = swap(back, COLUMN)
    grad_shard = scatter_rows(asked, returned)

    me = place(SUMMERS).reshape(1)
    piece = pair_scatter_sum(weight_pieces(me, features, grad_pre, extra), SUMMERS)
    low = pair_gather(sum_over_z(piece), SUMMERS[1:])
    grad_w, grad_b, grad_out = unpack(me, low, partner(low, SUMMERS[0]))
    return grad_shard[None], grad_w, grad_b.reshape(HIDDEN), grad_out.reshape(HIDDEN)


def solution(mesh):
    split = Mesh(mesh.devices.reshape((2,) * 10), (*COLUMN, *DP))
    return jax.shard_map(
        shards,
        mesh=split,
        in_specs=(
            P(None, COLUMN, None),
            P(COLUMN, DP, None, None, None),
            P(COLUMN, DP, None, None),
            P(COLUMN, DP, None, None),
            P(COLUMN, DP, None, None),
            P((*COLUMN, *DP)),
            P(),
            P(),
            P(),
        ),
        out_specs=(P(DP, None, COLUMN, None), P(), P(), P()),
        check_vma=False,
    )
```

```python
import jax
import jax.numpy as jnp
from jax import lax
from jax.experimental import pallas as pl
from jax.experimental.pallas import tpu as pltpu
from jax.sharding import Mesh, PartitionSpec as P

F32 = jnp.float32
BF16 = jnp.bfloat16
LANES = 128
TABLES = 3
ROWS_DEV = 256
WIDTH = 256
CAP = 8
N_FAR = 4
N_MID = 4
N_NEAR = 2
N_CORE = 2
N_DP = 16
N_Z = N_FAR * N_MID * N_NEAR
N_HELD = N_FAR * N_MID
N_TABLE = N_Z * N_CORE
LAYER = N_CORE * N_DP
GROUP = N_NEAR * LAYER
REQUEST_ROWS = 8
SLICE = WIDTH // N_DP
PACK = LANES // SLICE
BLOCKS = N_HELD // PACK
SAMPLES = 512
SLOTS = 2048
UNIQUE = N_TABLE * CAP
HIDDEN = 512
FEATURES = TABLES * WIDTH
TOKENS = SAMPLES * N_TABLE * N_DP
LANE_BLOCKS = HIDDEN // LANES
PIECE = FEATURES // (GROUP // 2)
HALF_BLOCKS = LANE_BLOCKS // 2
PIECE_ROWS = PIECE * HALF_BLOCKS
SUM_ROWS = PIECE_ROWS + 8
FAR = ("far1", "far0")
MID = ("mid1", "mid0")
COLUMN = (*FAR, *MID, "near", "core")
DP = ("x1", "x0", "y1", "y0")
SERVERS = ("near", "core", *DP)
SUMMERS = ("core", "y0", "x0", "y1", "x1", "near")
CHUNK = 32
VMEM = 56 * 1024 * 1024
LESS_VMEM = 16 * 1024 * 1024


def params(limit=VMEM):
    return pltpu.CompilerParams(vmem_limit_bytes=limit)


def two_parts(x):
    high = x.astype(BF16)
    return high, (x - high.astype(F32)).astype(BF16)


def dot(a, b, dims=((1,), (0,))):
    return lax.dot_general(a, b, (dims, ((), ())), preferred_element_type=F32)


def slice_kernel(dp_ref, table_ref, request_ref, out_ref, turned):
    dp = dp_ref[0]
    half = pl.multiple_of(dp // PACK * LANES, LANES)
    first = pl.multiple_of(dp % PACK * SLICE, SLICE)
    for t in range(TABLES):
        turned[...] = table_ref[t, :, pl.ds(half, LANES)].T
        for far in range(N_FAR):
            out_ref[far, t * SLICE : (t + 1) * SLICE] = turned[pl.ds(first, SLICE), :]
    for far in range(N_FAR):
        out_ref[far, TABLES * SLICE :, :LANES] = request_ref[:REQUEST_ROWS]
        out_ref[far, TABLES * SLICE :, LANES:] = request_ref[REQUEST_ROWS:]


def slice_rows(dp, emb_table, requests):
    whole = pl.BlockSpec(memory_space=pltpu.VMEM)
    return pl.pallas_call(
        slice_kernel,
        out_shape=jax.ShapeDtypeStruct((N_FAR, TABLES * SLICE + REQUEST_ROWS, ROWS_DEV), F32),
        in_specs=[pl.BlockSpec(memory_space=pltpu.SMEM), whole, whole],
        out_specs=whole,
        scratch_shapes=[pltpu.VMEM((LANES, ROWS_DEV), F32)],
        compiler_params=params(),
        name="slice_rows",
    )(dp, emb_table, requests)


def server_offset(i):
    return i ^ ((i >> 1) & 0b000101)


def serve_kernel(me_ref, mid_ref, ids_ref, slab_ref, out_ref):
    asked = GROUP * CAP
    ids = ids_ref[:, 0].reshape(asked, N_HELD)
    row = lax.broadcasted_iota(jnp.int32, (asked, ROWS_DEV), 1)
    group = lax.broadcasted_iota(jnp.int32, (asked, LANES), 1) // SLICE
    for block in range(BLOCKS):
        mids = range(block * PACK // N_FAR, (block + 1) * PACK // N_FAR)
        slab = [slab_ref[(mid + N_MID - mid_ref[0]) % N_MID].reshape(N_FAR * SLICE, ROWS_DEV) for mid in mids]
        slab = jnp.concatenate(slab).T
        stack = jnp.concatenate(two_parts(slab), axis=1)
        total = jnp.zeros((asked, LANES), F32)
        for owner in range(PACK):
            z = block * PACK + owner
            onehot = jnp.where(ids[:, z : z + 1] == row, 1.0, 0.0).astype(BF16)
            both = dot(onehot, stack)
            total = jnp.where(group == owner, both[:, :LANES] + both[:, LANES:], total)
        for i in range(GROUP):
            out_ref[me_ref[0] ^ server_offset(i), 0, block] = total[i * CAP : (i + 1) * CAP]


def serve_rows(me, mid, ids, slab):
    return pl.pallas_call(
        serve_kernel,
        grid=(TABLES,),
        out_shape=jax.ShapeDtypeStruct((GROUP, TABLES, BLOCKS, CAP, LANES), F32),
        in_specs=[
            pl.BlockSpec(memory_space=pltpu.SMEM),
            pl.BlockSpec(memory_space=pltpu.SMEM),
            pl.BlockSpec((GROUP, 1, CAP, N_HELD), lambda t: (0, t, 0, 0)),
            pl.BlockSpec((N_MID, N_FAR, SLICE, ROWS_DEV), lambda t: (0, 0, t, 0)),
        ],
        out_specs=pl.BlockSpec((GROUP, 1, BLOCKS, CAP, LANES), lambda t: (0, t, 0, 0, 0)),
        compiler_params=params(),
        name="serve_rows",
    )(me, mid, ids, slab)


def count_kernel(inverse_ref, bag_ref, live_ref, count_ref, turned_ref):
    sample = lax.broadcasted_iota(jnp.int32, (SAMPLES, SLOTS), 0)
    unique = lax.broadcasted_iota(jnp.int32, (UNIQUE, SLOTS), 0)
    in_bag = jnp.where(sample == bag_ref[0], 1.0, 0.0).astype(BF16)
    in_slot = jnp.where(unique == inverse_ref[0], 1.0, 0.0).astype(BF16)
    counts = dot(in_bag, in_slot, ((1,), (1,)))
    count_ref[0] = (counts * live_ref[0]).astype(BF16)
    turned_ref[0] = counts.T.astype(BF16)


def count_slots(inverse, bag_ids, live):
    row = lambda t: (t, 0, 0)
    return pl.pallas_call(
        count_kernel,
        grid=(TABLES,),
        out_shape=[
            jax.ShapeDtypeStruct((TABLES, SAMPLES, UNIQUE), BF16),
            jax.ShapeDtypeStruct((TABLES, UNIQUE, SAMPLES), BF16),
        ],
        in_specs=[
            pl.BlockSpec((1, 1, SLOTS), row),
            pl.BlockSpec((1, 1, SLOTS), row),
            pl.BlockSpec((1, 1, UNIQUE), row),
        ],
        out_specs=[
            pl.BlockSpec((1, SAMPLES, UNIQUE), row),
            pl.BlockSpec((1, UNIQUE, SAMPLES), row),
        ],
        compiler_params=params(),
        name="count_slots",
    )(inverse, bag_ids, live)


def exchange_groups(tiles):
    group = lax.broadcasted_iota(jnp.int32, tiles[0].shape, 1) // SLICE
    step = PACK // 2
    while step:
        low_half = (group & step) == 0
        swapped = list(tiles)
        for i in range(PACK):
            if i & step == 0:
                a, b = tiles[i], tiles[i + step]
                swapped[i] = jnp.where(low_half, a, pltpu.roll(b, step * SLICE, 1))
                swapped[i + step] = jnp.where(low_half, pltpu.roll(a, LANES - step * SLICE, 1), b)
        tiles = swapped
        step //= 2
    return tiles


def tower_kernel(fetched_ref, count_ref, turned_ref, w_hidden_ref, bias_ref, w_out_ref, label_ref,
                 back_ref, feature_ref, grad_pre_ref, extra_ref, unique, pre):
    for t in range(TABLES):
        for source in range(N_NEAR * N_CORE):
            for half in range(N_DP // PACK):
                first = source * N_DP + half * PACK
                tiles = [fetched_ref[first + i, t].reshape(BLOCKS * CAP, LANES) for i in range(PACK)]
                for owner, tile in enumerate(exchange_groups(tiles)):
                    held = tile.reshape(BLOCKS, CAP, LANES)
                    for block in range(BLOCKS):
                        mid, far = divmod(block * PACK + owner, N_FAR)
                        unique[far, mid, source, :, half * LANES : (half + 1) * LANES] = held[block]
        high, low = two_parts(unique[...].reshape(UNIQUE, WIDTH))
        counts = count_ref[t]
        pooled = dot(counts, high) + dot(counts, low)
        feature_ref[:, t * WIDTH : (t + 1) * WIDTH] = pooled.astype(BF16)
    pre[...] = dot(feature_ref[...], w_hidden_ref[...]) + bias_ref[...]

    def chunk(i, sums):
        rows = pl.ds(pl.multiple_of(i * CHUNK, CHUNK), CHUNK)
        w_out = w_out_ref[...]
        x = pre[rows, :]
        sigma = jax.nn.sigmoid(x)
        hidden = x * sigma
        logit = jnp.sum(hidden * w_out, axis=1, keepdims=True)
        error = jax.nn.sigmoid(logit) - label_ref[rows, :].astype(F32)
        grad_pre = error * w_out * sigma * (1.0 + x * (1.0 - sigma))
        grad_pre_ref[rows, :] = grad_pre.astype(BF16)
        fold = lambda v: jnp.sum(v.reshape(CHUNK // 8, 8, HIDDEN), axis=0)
        return sums[0] + fold(grad_pre), sums[1] + fold(error * hidden)

    start = jnp.zeros((8, HIDDEN), F32)
    sums = lax.fori_loop(0, SAMPLES // CHUNK, chunk, (start, start))
    for which in range(2):
        row = jnp.sum(sums[which], axis=0, keepdims=True)
        for block in range(LANE_BLOCKS):
            at = which * LANE_BLOCKS + block
            extra_ref[at : at + 1, :] = row[:, block * LANES : (block + 1) * LANES]
    grad_pre = grad_pre_ref[...]
    for t in range(TABLES):
        grad = dot(grad_pre, w_hidden_ref[t * WIDTH : (t + 1) * WIDTH, :], ((1,), (1,)))
        high, low = two_parts(grad)
        turned = turned_ref[t]
        back_ref[:, t] = (dot(turned, high) + dot(turned, low)).reshape(N_TABLE, CAP, WIDTH)


def tower(fetched, counts, turned, w_hidden, b_hidden, w_out, labels):
    whole = pl.BlockSpec(memory_space=pltpu.VMEM)
    return pl.pallas_call(
        tower_kernel,
        out_shape=[
            jax.ShapeDtypeStruct((N_TABLE, TABLES, CAP, WIDTH), F32),
            jax.ShapeDtypeStruct((SAMPLES, FEATURES), BF16),
            jax.ShapeDtypeStruct((SAMPLES, HIDDEN), BF16),
            jax.ShapeDtypeStruct((8, LANES), F32),
        ],
        in_specs=[whole] * 7,
        out_specs=[whole] * 4,
        scratch_shapes=[
            pltpu.VMEM((N_FAR, N_MID, N_NEAR * N_CORE, CAP, WIDTH), F32),
            pltpu.VMEM((SAMPLES, HIDDEN), F32),
        ],
        compiler_params=params(),
        name="tower",
    )(fetched, counts, turned, w_hidden, b_hidden, w_out, labels)


def piece_at(piece, block):
    rows = pl.ds(pl.multiple_of((piece >> 1) * PIECE, 8), PIECE)
    columns = pl.ds(pl.multiple_of(((piece & 1) * HALF_BLOCKS + block) * LANES, LANES), LANES)
    return rows, columns


def weight_kernel(me_ref, feature_ref, grad_pre_ref, extra_ref, out_ref, grad):
    grad[...] = dot(feature_ref[...], grad_pre_ref[...], ((0,), (0,)))
    for i in range(GROUP):
        for block in range(HALF_BLOCKS):
            rows, columns = piece_at(me_ref[0] ^ i, block)
            out_ref[i, block * PIECE : (block + 1) * PIECE, :] = grad[rows, columns]
        out_ref[i, PIECE_ROWS:, :] = extra_ref[...]


def weight_pieces(me, features, grad_pre, extra):
    whole = pl.BlockSpec(memory_space=pltpu.VMEM)
    return pl.pallas_call(
        weight_kernel,
        out_shape=jax.ShapeDtypeStruct((GROUP, SUM_ROWS, LANES), F32),
        in_specs=[pl.BlockSpec(memory_space=pltpu.SMEM)] + [whole] * 3,
        out_specs=whole,
        scratch_shapes=[pltpu.VMEM((FEATURES, HIDDEN), F32)],
        compiler_params=params(),
        name="weight_pieces",
    )(me, features, grad_pre, extra)


def unpack_kernel(me_ref, low_ref, high_ref, w_hidden_ref, bias_ref, w_out_ref):
    for i in range(GROUP):
        piece_ref = high_ref if i >= GROUP // 2 else low_ref
        for block in range(HALF_BLOCKS):
            rows, columns = piece_at(me_ref[0] ^ i, block)
            w_hidden_ref[rows, columns] = (
                piece_ref[i % (GROUP // 2), block * PIECE : (block + 1) * PIECE, :] / TOKENS
            )
    for block in range(LANE_BLOCKS):
        at = PIECE_ROWS + block
        columns = pl.ds(block * LANES, LANES)
        bias_ref[:, columns] = low_ref[0, at : at + 1, :] / TOKENS
        at = at + LANE_BLOCKS
        w_out_ref[:, columns] = low_ref[0, at : at + 1, :] / TOKENS


def unpack(me, low, high):
    whole = pl.BlockSpec(memory_space=pltpu.VMEM)
    return pl.pallas_call(
        unpack_kernel,
        out_shape=[
            jax.ShapeDtypeStruct((FEATURES, HIDDEN), F32),
            jax.ShapeDtypeStruct((1, HIDDEN), F32),
            jax.ShapeDtypeStruct((1, HIDDEN), F32),
        ],
        in_specs=[pl.BlockSpec(memory_space=pltpu.SMEM)] + [whole] * 2,
        out_specs=[whole] * 3,
        compiler_params=params(LESS_VMEM),
        name="unpack",
    )(me, low, high)


def scatter_kernel(ids_ref, returned_ref, out_ref):
    row = lax.broadcasted_iota(jnp.int32, (ROWS_DEV, UNIQUE), 0)
    onehot = jnp.where(row == ids_ref[0], 1.0, 0.0).astype(BF16)
    high, low = two_parts(returned_ref[:, 0].reshape(UNIQUE, WIDTH))
    out_ref[0] = dot(onehot, high) + dot(onehot, low)


def scatter_rows(ids, returned):
    return pl.pallas_call(
        scatter_kernel,
        grid=(TABLES,),
        out_shape=jax.ShapeDtypeStruct((TABLES, ROWS_DEV, WIDTH), F32),
        in_specs=[
            pl.BlockSpec((1, 1, UNIQUE), lambda t: (t, 0, 0)),
            pl.BlockSpec((N_TABLE, 1, CAP, WIDTH), lambda t: (0, t, 0, 0)),
        ],
        out_specs=pl.BlockSpec((1, ROWS_DEV, WIDTH), lambda t: (t, 0, 0)),
        compiler_params=params(LESS_VMEM),
        name="scatter_rows",
    )(ids, returned)


def place(axes):
    return lax.axis_index(axes)


def swap(x, axes):
    return lax.all_to_all(x, axes, split_axis=0, concat_axis=0, tiled=True)


def partner(x, axis):
    if axis in ("x1", "y1"):
        return lax.ppermute(x, (axis, axis[0] + "0"), [(i, 3 - i) for i in range(4)])
    return lax.ppermute(x, axis, [(0, 1), (1, 0)])


def pair_place(axes):
    index = 0
    for axis in axes:
        bit = lax.axis_index(axis)
        if axis in ("x0", "y0"):
            bit = bit ^ lax.axis_index(axis[0] + "1")
        index = index * 2 + bit
    return index


def pair_swap(x, axes):
    half = x.shape[0] // 2
    for axis in axes:
        x = jnp.stack([x[:half], partner(x[half:], axis)], axis=1).reshape(x.shape)
    return x


def pair_gather(x, axes):
    for axis in reversed(axes):
        x = jnp.concatenate([x, partner(x, axis)])
    return x


def relative(x, axes):
    shape = x.shape
    for at, axis in enumerate(axes):
        x = x.reshape(2**at, 2, -1, *shape[1:])
        x = jnp.where(lax.axis_index(axis) == 1, x[:, ::-1], x)
    return x.reshape(shape)


def pair_scatter_sum(x, axes):
    for axis in axes:
        half = x.shape[0] // 2
        x = x[:half] + partner(x[half:], axis)
    return x[0]


def shift(x, axes, count, by):
    return lax.ppermute(x, axes, [(i, (i + by) % count) for i in range(count)])


def sum_over_z(x):
    for axis in reversed(MID):
        x = x + partner(x, axis)
    x = x + partner(x, FAR[1])
    return x + lax.ppermute(x, FAR, [(i, N_FAR - 1 - i) for i in range(N_FAR)])


def shards(emb_table, row_request, live_count, inverse, bag_ids, labels, w_hidden, b_hidden, w_out):
    request = row_request[0, 0]

    near = N_NEAR * N_CORE
    grouped = jnp.transpose(request.reshape(TABLES, N_FAR, N_MID, near, CAP), (3, 0, 4, 2, 1))
    grouped = relative(grouped.reshape(near, TABLES, CAP * N_HELD), ("near", "core"))
    grouped = pair_swap(grouped, ("near", "core"))
    ids = jnp.swapaxes(pair_gather(grouped[None], DP), 0, 1).reshape(GROUP, TABLES, CAP, N_HELD)

    travel = grouped.reshape(near * TABLES, CAP * N_HELD).astype(F32)
    travel = jnp.pad(travel, ((0, 2 * REQUEST_ROWS - near * TABLES), (0, 0)))
    slab = swap(slice_rows(place(DP).reshape(1), emb_table, travel), FAR)
    slab, ids = lax.optimization_barrier((slab, ids))
    held = (*FAR, *MID)
    across = [shift(slab[: N_FAR // 2], held, N_HELD, -2), shift(slab[N_FAR // 2 :], held, N_HELD, 2)]
    slab = jnp.stack([slab, shift(slab, held, N_HELD, -1), jnp.concatenate(across), shift(slab, held, N_HELD, 1)])

    mid = place(MID)
    asked = slab[:, :, TABLES * SLICE :]
    asked = jnp.concatenate([asked[..., :LANES], asked[..., LANES:]], axis=2)[:, :, : near * TABLES]
    asked = asked.reshape(N_MID, N_FAR, near, TABLES, CAP, N_HELD)
    asked = lax.dynamic_index_in_dim(asked, mid * N_FAR + place(FAR), 5, keepdims=False).astype(jnp.int32)
    asked = lax.dynamic_slice_in_dim(jnp.concatenate([asked, asked]), (N_MID - mid) % N_MID, N_MID, axis=0)
    asked = relative(jnp.moveaxis(asked, 2, 0), ("near", "core"))
    asked = jnp.transpose(asked, (3, 2, 1, 0, 4)).reshape(TABLES, 1, UNIQUE)

    slot = lax.broadcasted_iota(jnp.int32, (TABLES, N_TABLE, CAP), 2)
    live = (slot < live_count[0, 0][:, :, None]).astype(F32).reshape(TABLES, 1, UNIQUE)
    counts, turned = count_slots(
        inverse[0, 0].reshape(TABLES, 1, SLOTS), bag_ids[0, 0].reshape(TABLES, 1, SLOTS), live
    )

    slab, counts, turned = lax.optimization_barrier((slab, counts, turned))
    fetched = swap(serve_rows(place(SERVERS).reshape(1), mid.reshape(1), ids, slab), SERVERS)
    fetched, asked = lax.optimization_barrier((fetched, asked))
    back, features, grad_pre, extra = tower(
        fetched,
        counts,
        turned,
        w_hidden,
        b_hidden.reshape(1, HIDDEN),
        w_out.reshape(1, HIDDEN),
        labels.reshape(SAMPLES, 1),
    )
    grad_shard = scatter_rows(asked, swap(back, COLUMN))
    me = pair_place(SUMMERS).reshape(1)
    piece = pair_scatter_sum(weight_pieces(me, features, grad_pre, extra), SUMMERS)
    low = pair_gather(sum_over_z(piece)[None], SUMMERS[1:])
    high, grad_shard = lax.optimization_barrier((partner(low, SUMMERS[0]), grad_shard))
    grad_w, grad_b, grad_out = unpack(me, low, high)
    return grad_shard[None], grad_w, grad_b.reshape(HIDDEN), grad_out.reshape(HIDDEN)


def solution(mesh):
    split = Mesh(mesh.devices.reshape((2,) * 10), (*COLUMN, *DP))
    return jax.shard_map(
        shards,
        mesh=split,
        in_specs=(
            P(None, COLUMN, None),
            P(COLUMN, DP, None, None, None),
            P(COLUMN, DP, None, None),
            P(COLUMN, DP, None, None),
            P(COLUMN, DP, None, None),
            P((*COLUMN, *DP)),
            P(),
            P(),
            P(),
        ),
        out_specs=(P(DP, None, COLUMN, None), P(), P(), P()),
        check_vma=False,
    )
```

```python
import jax
import jax.numpy as jnp
from jax import lax
from jax.experimental import pallas as pl
from jax.experimental.pallas import tpu as pltpu
from jax.sharding import Mesh, PartitionSpec as P

F32 = jnp.float32
BF16 = jnp.bfloat16
LANES = 128
TABLES = 3
ROWS_DEV = 256
WIDTH = 256
CAP = 8
N_FAR = 4
N_MID = 4
N_NEAR = 2
N_CORE = 2
N_DP = 16
N_Z = N_FAR * N_MID * N_NEAR
N_HELD = N_FAR * N_MID
N_TABLE = N_Z * N_CORE
LAYER = N_CORE * N_DP
GROUP = N_NEAR * LAYER
REQUEST_ROWS = 8
SLICE = WIDTH // N_DP
PACK = LANES // SLICE
BLOCKS = N_HELD // PACK
SAMPLES = 512
SLOTS = 2048
UNIQUE = N_TABLE * CAP
HIDDEN = 512
FEATURES = TABLES * WIDTH
TOKENS = SAMPLES * N_TABLE * N_DP
LANE_BLOCKS = HIDDEN // LANES
PIECE = FEATURES // (GROUP // 2)
HALF_BLOCKS = LANE_BLOCKS // 2
PIECE_ROWS = PIECE * HALF_BLOCKS
SUM_ROWS = PIECE_ROWS + 8
FAR = ("far1", "far0")
MID = ("mid1", "mid0")
COLUMN = (*FAR, *MID, "near", "core")
DP = ("x1", "x0", "y1", "y0")
SERVERS = ("near", "core", *DP)
SUMMERS = ("core", "y1", "y0", "x1", "x0", "near")
CHUNK = 32
VMEM = 56 * 1024 * 1024
LESS_VMEM = 16 * 1024 * 1024


def params(limit=VMEM):
    return pltpu.CompilerParams(vmem_limit_bytes=limit)


def two_parts(x):
    high = x.astype(BF16)
    return high, (x - high.astype(F32)).astype(BF16)


def dot(a, b, dims=((1,), (0,))):
    return lax.dot_general(a, b, (dims, ((), ())), preferred_element_type=F32)


def slice_kernel(dp_ref, table_ref, request_ref, out_ref, turned):
    dp = dp_ref[0]
    half = pl.multiple_of(dp // PACK * LANES, LANES)
    first = pl.multiple_of(dp % PACK * SLICE, SLICE)
    for t in range(TABLES):
        turned[...] = table_ref[t, :, pl.ds(half, LANES)].T
        for far in range(N_FAR):
            out_ref[far, t * SLICE : (t + 1) * SLICE] = turned[pl.ds(first, SLICE), :]
    for far in range(N_FAR):
        out_ref[far, TABLES * SLICE :, :LANES] = request_ref[:REQUEST_ROWS]
        out_ref[far, TABLES * SLICE :, LANES:] = request_ref[REQUEST_ROWS:]


def slice_rows(dp, emb_table, requests):
    whole = pl.BlockSpec(memory_space=pltpu.VMEM)
    return pl.pallas_call(
        slice_kernel,
        out_shape=jax.ShapeDtypeStruct((N_FAR, TABLES * SLICE + REQUEST_ROWS, ROWS_DEV), F32),
        in_specs=[pl.BlockSpec(memory_space=pltpu.SMEM), whole, whole],
        out_specs=whole,
        scratch_shapes=[pltpu.VMEM((LANES, ROWS_DEV), F32)],
        compiler_params=params(),
        name="slice_rows",
    )(dp, emb_table, requests)


def server_offset(i):
    return i ^ ((i >> 1) & 0b000101)


def serve_kernel(me_ref, mid_ref, ids_ref, slab_ref, out_ref):
    asked = GROUP * CAP
    ids = ids_ref[:, 0].reshape(asked, N_HELD)
    row = lax.broadcasted_iota(jnp.int32, (asked, ROWS_DEV), 1)
    group = lax.broadcasted_iota(jnp.int32, (asked, LANES), 1) // SLICE
    for block in range(BLOCKS):
        mids = range(block * PACK // N_FAR, (block + 1) * PACK // N_FAR)
        slab = [slab_ref[(mid + N_MID - mid_ref[0]) % N_MID].reshape(N_FAR * SLICE, ROWS_DEV) for mid in mids]
        slab = jnp.concatenate(slab).T
        stack = jnp.concatenate(two_parts(slab), axis=1)
        total = jnp.zeros((asked, LANES), F32)
        for owner in range(PACK):
            z = block * PACK + owner
            onehot = jnp.where(ids[:, z : z + 1] == row, 1.0, 0.0).astype(BF16)
            both = dot(onehot, stack)
            total = jnp.where(group == owner, both[:, :LANES] + both[:, LANES:], total)
        for i in range(GROUP):
            out_ref[me_ref[0] ^ server_offset(i), 0, block] = total[i * CAP : (i + 1) * CAP]


def serve_rows(me, mid, ids, slab):
    return pl.pallas_call(
        serve_kernel,
        grid=(TABLES,),
        out_shape=jax.ShapeDtypeStruct((GROUP, TABLES, BLOCKS, CAP, LANES), F32),
        in_specs=[
            pl.BlockSpec(memory_space=pltpu.SMEM),
            pl.BlockSpec(memory_space=pltpu.SMEM),
            pl.BlockSpec((GROUP, 1, CAP, N_HELD), lambda t: (0, t, 0, 0)),
            pl.BlockSpec((N_MID, N_FAR, SLICE, ROWS_DEV), lambda t: (0, 0, t, 0)),
        ],
        out_specs=pl.BlockSpec((GROUP, 1, BLOCKS, CAP, LANES), lambda t: (0, t, 0, 0, 0)),
        compiler_params=params(),
        name="serve_rows",
    )(me, mid, ids, slab)


def count_kernel(inverse_ref, bag_ref, live_ref, count_ref, turned_ref):
    sample = lax.broadcasted_iota(jnp.int32, (SAMPLES, SLOTS), 0)
    unique = lax.broadcasted_iota(jnp.int32, (UNIQUE, SLOTS), 0)
    in_bag = jnp.where(sample == bag_ref[0], 1.0, 0.0).astype(BF16)
    in_slot = jnp.where(unique == inverse_ref[0], 1.0, 0.0).astype(BF16)
    counts = dot(in_bag, in_slot, ((1,), (1,)))
    count_ref[0] = (counts * live_ref[0]).astype(BF16)
    turned_ref[0] = counts.T.astype(BF16)


def count_slots(inverse, bag_ids, live):
    row = lambda t: (t, 0, 0)
    return pl.pallas_call(
        count_kernel,
        grid=(TABLES,),
        out_shape=[
            jax.ShapeDtypeStruct((TABLES, SAMPLES, UNIQUE), BF16),
            jax.ShapeDtypeStruct((TABLES, UNIQUE, SAMPLES), BF16),
        ],
        in_specs=[
            pl.BlockSpec((1, 1, SLOTS), row),
            pl.BlockSpec((1, 1, SLOTS), row),
            pl.BlockSpec((1, 1, UNIQUE), row),
        ],
        out_specs=[
            pl.BlockSpec((1, SAMPLES, UNIQUE), row),
            pl.BlockSpec((1, UNIQUE, SAMPLES), row),
        ],
        compiler_params=params(),
        name="count_slots",
    )(inverse, bag_ids, live)


def exchange_groups(tiles):
    group = lax.broadcasted_iota(jnp.int32, tiles[0].shape, 1) // SLICE
    step = PACK // 2
    while step:
        low_half = (group & step) == 0
        swapped = list(tiles)
        for i in range(PACK):
            if i & step == 0:
                a, b = tiles[i], tiles[i + step]
                swapped[i] = jnp.where(low_half, a, pltpu.roll(b, step * SLICE, 1))
                swapped[i + step] = jnp.where(low_half, pltpu.roll(a, LANES - step * SLICE, 1), b)
        tiles = swapped
        step //= 2
    return tiles


def tower_kernel(fetched_ref, count_ref, turned_ref, w_hidden_ref, bias_ref, w_out_ref, label_ref,
                 back_ref, feature_ref, grad_pre_ref, extra_ref, unique, pre):
    for t in range(TABLES):
        for source in range(N_NEAR * N_CORE):
            for half in range(N_DP // PACK):
                first = source * N_DP + half * PACK
                tiles = [fetched_ref[first + i, t].reshape(BLOCKS * CAP, LANES) for i in range(PACK)]
                for owner, tile in enumerate(exchange_groups(tiles)):
                    held = tile.reshape(BLOCKS, CAP, LANES)
                    for block in range(BLOCKS):
                        mid, far = divmod(block * PACK + owner, N_FAR)
                        unique[far, mid, source, :, half * LANES : (half + 1) * LANES] = held[block]
        high, low = two_parts(unique[...].reshape(UNIQUE, WIDTH))
        counts = count_ref[t]
        pooled = dot(counts, high) + dot(counts, low)
        feature_ref[:, t * WIDTH : (t + 1) * WIDTH] = pooled.astype(BF16)
    pre[...] = dot(feature_ref[...], w_hidden_ref[...]) + bias_ref[...]

    def chunk(i, sums):
        rows = pl.ds(pl.multiple_of(i * CHUNK, CHUNK), CHUNK)
        w_out = w_out_ref[...]
        x = pre[rows, :]
        sigma = jax.nn.sigmoid(x)
        hidden = x * sigma
        logit = jnp.sum(hidden * w_out, axis=1, keepdims=True)
        error = jax.nn.sigmoid(logit) - label_ref[rows, :].astype(F32)
        grad_pre = error * w_out * sigma * (1.0 + x * (1.0 - sigma))
        grad_pre_ref[rows, :] = grad_pre.astype(BF16)
        fold = lambda v: jnp.sum(v.reshape(CHUNK // 8, 8, HIDDEN), axis=0)
        return sums[0] + fold(grad_pre), sums[1] + fold(error * hidden)

    start = jnp.zeros((8, HIDDEN), F32)
    sums = lax.fori_loop(0, SAMPLES // CHUNK, chunk, (start, start))
    for which in range(2):
        row = jnp.sum(sums[which], axis=0, keepdims=True)
        for block in range(LANE_BLOCKS):
            at = which * LANE_BLOCKS + block
            extra_ref[at : at + 1, :] = row[:, block * LANES : (block + 1) * LANES]
    grad_pre = grad_pre_ref[...]
    for t in range(TABLES):
        grad = dot(grad_pre, w_hidden_ref[t * WIDTH : (t + 1) * WIDTH, :], ((1,), (1,)))
        high, low = two_parts(grad)
        turned = turned_ref[t]
        back_ref[:, t] = (dot(turned, high) + dot(turned, low)).reshape(N_TABLE, CAP, WIDTH)


def tower(fetched, counts, turned, w_hidden, b_hidden, w_out, labels):
    whole = pl.BlockSpec(memory_space=pltpu.VMEM)
    return pl.pallas_call(
        tower_kernel,
        out_shape=[
            jax.ShapeDtypeStruct((N_TABLE, TABLES, CAP, WIDTH), F32),
            jax.ShapeDtypeStruct((SAMPLES, FEATURES), BF16),
            jax.ShapeDtypeStruct((SAMPLES, HIDDEN), BF16),
            jax.ShapeDtypeStruct((8, LANES), F32),
        ],
        in_specs=[whole] * 7,
        out_specs=[whole] * 4,
        scratch_shapes=[
            pltpu.VMEM((N_FAR, N_MID, N_NEAR * N_CORE, CAP, WIDTH), F32),
            pltpu.VMEM((SAMPLES, HIDDEN), F32),
        ],
        compiler_params=params(),
        name="tower",
    )(fetched, counts, turned, w_hidden, b_hidden, w_out, labels)


def piece_at(piece, block):
    rows = pl.ds(pl.multiple_of((piece >> 1) * PIECE, 8), PIECE)
    columns = pl.ds(pl.multiple_of(((piece & 1) * HALF_BLOCKS + block) * LANES, LANES), LANES)
    return rows, columns


def weight_kernel(me_ref, feature_ref, grad_pre_ref, extra_ref, out_ref, grad):
    grad[...] = dot(feature_ref[...], grad_pre_ref[...], ((0,), (0,)))
    for i in range(GROUP):
        for block in range(HALF_BLOCKS):
            rows, columns = piece_at(me_ref[0] ^ i, block)
            out_ref[i, block * PIECE : (block + 1) * PIECE, :] = grad[rows, columns]
        out_ref[i, PIECE_ROWS:, :] = extra_ref[...]


def weight_pieces(me, features, grad_pre, extra):
    whole = pl.BlockSpec(memory_space=pltpu.VMEM)
    return pl.pallas_call(
        weight_kernel,
        out_shape=jax.ShapeDtypeStruct((GROUP, SUM_ROWS, LANES), F32),
        in_specs=[pl.BlockSpec(memory_space=pltpu.SMEM)] + [whole] * 3,
        out_specs=whole,
        scratch_shapes=[pltpu.VMEM((FEATURES, HIDDEN), F32)],
        compiler_params=params(),
        name="weight_pieces",
    )(me, features, grad_pre, extra)


def unpack_kernel(me_ref, low_ref, high_ref, w_hidden_ref, bias_ref, w_out_ref):
    for i in range(GROUP):
        piece_ref = high_ref if i >= GROUP // 2 else low_ref
        for block in range(HALF_BLOCKS):
            rows, columns = piece_at(me_ref[0] ^ i, block)
            w_hidden_ref[rows, columns] = (
                piece_ref[i % (GROUP // 2), block * PIECE : (block + 1) * PIECE, :] / TOKENS
            )
    for block in range(LANE_BLOCKS):
        at = PIECE_ROWS + block
        columns = pl.ds(block * LANES, LANES)
        bias_ref[:, columns] = low_ref[0, at : at + 1, :] / TOKENS
        at = at + LANE_BLOCKS
        w_out_ref[:, columns] = low_ref[0, at : at + 1, :] / TOKENS


def unpack(me, low, high):
    whole = pl.BlockSpec(memory_space=pltpu.VMEM)
    return pl.pallas_call(
        unpack_kernel,
        out_shape=[
            jax.ShapeDtypeStruct((FEATURES, HIDDEN), F32),
            jax.ShapeDtypeStruct((1, HIDDEN), F32),
            jax.ShapeDtypeStruct((1, HIDDEN), F32),
        ],
        in_specs=[pl.BlockSpec(memory_space=pltpu.SMEM)] + [whole] * 2,
        out_specs=[whole] * 3,
        compiler_params=params(LESS_VMEM),
        name="unpack",
    )(me, low, high)


def scatter_kernel(ids_ref, returned_ref, out_ref):
    row = lax.broadcasted_iota(jnp.int32, (ROWS_DEV, UNIQUE), 0)
    onehot = jnp.where(row == ids_ref[0], 1.0, 0.0).astype(BF16)
    high, low = two_parts(returned_ref[:, 0].reshape(UNIQUE, WIDTH))
    out_ref[0] = dot(onehot, high) + dot(onehot, low)


def scatter_rows(ids, returned):
    return pl.pallas_call(
        scatter_kernel,
        grid=(TABLES,),
        out_shape=jax.ShapeDtypeStruct((TABLES, ROWS_DEV, WIDTH), F32),
        in_specs=[
            pl.BlockSpec((1, 1, UNIQUE), lambda t: (t, 0, 0)),
            pl.BlockSpec((N_TABLE, 1, CAP, WIDTH), lambda t: (0, t, 0, 0)),
        ],
        out_specs=pl.BlockSpec((1, ROWS_DEV, WIDTH), lambda t: (t, 0, 0)),
        compiler_params=params(LESS_VMEM),
        name="scatter_rows",
    )(ids, returned)


def place(axes):
    return lax.axis_index(axes)


def swap(x, axes):
    return lax.all_to_all(x, axes, split_axis=0, concat_axis=0, tiled=True)


def partner(x, axis):
    if axis in ("x1", "y1"):
        return lax.ppermute(x, (axis, axis[0] + "0"), [(i, 3 - i) for i in range(4)])
    return lax.ppermute(x, axis, [(0, 1), (1, 0)])


def pair_place(axes):
    index = 0
    for axis in axes:
        bit = lax.axis_index(axis)
        if axis in ("x0", "y0"):
            bit = bit ^ lax.axis_index(axis[0] + "1")
        index = index * 2 + bit
    return index


def pair_swap(x, axes):
    half = x.shape[0] // 2
    for axis in axes:
        x = jnp.stack([x[:half], partner(x[half:], axis)], axis=1).reshape(x.shape)
    return x


def pair_gather(x, axes):
    for axis in reversed(axes):
        x = jnp.concatenate([x, partner(x, axis)])
    return x


def ring_gather(x, ring):
    half = x.shape[0] // 2
    one, other = partner(x, ring + "0"), partner(x, ring + "1")
    opposite = [partner(other[:half], ring + "0"), partner(one[half:], ring + "1")]
    return jnp.concatenate([x, one, other, *opposite])


def relative(x, axes):
    shape = x.shape
    for at, axis in enumerate(axes):
        x = x.reshape(2**at, 2, -1, *shape[1:])
        x = jnp.where(lax.axis_index(axis) == 1, x[:, ::-1], x)
    return x.reshape(shape)


def pair_scatter_sum(x, axes):
    for axis in axes:
        half = x.shape[0] // 2
        x = x[:half] + partner(x[half:], axis)
    return x[0]


def shift(x, axes, count, by):
    return lax.ppermute(x, axes, [(i, (i + by) % count) for i in range(count)])


def sum_over_z(x):
    for axis in reversed(MID):
        x = x + partner(x, axis)
    x = x + partner(x, FAR[1])
    return x + lax.ppermute(x, FAR, [(i, N_FAR - 1 - i) for i in range(N_FAR)])


def shards(emb_table, row_request, live_count, inverse, bag_ids, labels, w_hidden, b_hidden, w_out):
    request = row_request[0, 0]

    near = N_NEAR * N_CORE
    grouped = jnp.transpose(request.reshape(TABLES, N_FAR, N_MID, near, CAP), (3, 0, 4, 2, 1))
    grouped = relative(grouped.reshape(near, TABLES, CAP * N_HELD), ("near", "core"))
    grouped = pair_swap(grouped, ("near", "core"))
    ids = jnp.swapaxes(pair_gather(grouped[None], DP), 0, 1).reshape(GROUP, TABLES, CAP, N_HELD)

    travel = grouped.reshape(near * TABLES, CAP * N_HELD).astype(F32)
    travel = jnp.pad(travel, ((0, 2 * REQUEST_ROWS - near * TABLES), (0, 0)))
    slab = swap(slice_rows(place(DP).reshape(1), emb_table, travel), FAR)
    slab, ids = lax.optimization_barrier((slab, ids))
    held = (*FAR, *MID)
    across = [shift(slab[: N_FAR // 2], held, N_HELD, -2), shift(slab[N_FAR // 2 :], held, N_HELD, 2)]
    slab = jnp.stack([slab, shift(slab, held, N_HELD, -1), jnp.concatenate(across), shift(slab, held, N_HELD, 1)])

    mid = place(MID)
    asked = slab[:, :, TABLES * SLICE :]
    asked = jnp.concatenate([asked[..., :LANES], asked[..., LANES:]], axis=2)[:, :, : near * TABLES]
    asked = asked.reshape(N_MID, N_FAR, near, TABLES, CAP, N_HELD)
    asked = lax.dynamic_index_in_dim(asked, mid * N_FAR + place(FAR), 5, keepdims=False).astype(jnp.int32)
    asked = lax.dynamic_slice_in_dim(jnp.concatenate([asked, asked]), (N_MID - mid) % N_MID, N_MID, axis=0)
    asked = relative(jnp.moveaxis(asked, 2, 0), ("near", "core"))
    asked = jnp.transpose(asked, (3, 2, 1, 0, 4)).reshape(TABLES, 1, UNIQUE)

    slot = lax.broadcasted_iota(jnp.int32, (TABLES, N_TABLE, CAP), 2)
    live = (slot < live_count[0, 0][:, :, None]).astype(F32).reshape(TABLES, 1, UNIQUE)
    counts, turned = count_slots(
        inverse[0, 0].reshape(TABLES, 1, SLOTS), bag_ids[0, 0].reshape(TABLES, 1, SLOTS), live
    )

    slab, counts, turned = lax.optimization_barrier((slab, counts, turned))
    fetched = swap(serve_rows(place(SERVERS).reshape(1), mid.reshape(1), ids, slab), SERVERS)
    fetched, asked = lax.optimization_barrier((fetched, asked))
    back, features, grad_pre, extra = tower(
        fetched,
        counts,
        turned,
        w_hidden,
        b_hidden.reshape(1, HIDDEN),
        w_out.reshape(1, HIDDEN),
        labels.reshape(SAMPLES, 1),
    )
    grad_shard = scatter_rows(asked, swap(back, COLUMN))
    me = pair_place(SUMMERS).reshape(1)
    piece = pair_scatter_sum(weight_pieces(me, features, grad_pre, extra), SUMMERS)
    low = pair_gather(sum_over_z(piece)[None], ("near",))
    low = ring_gather(ring_gather(low, "x"), "y")
    high, grad_shard = lax.optimization_barrier((partner(low, SUMMERS[0]), grad_shard))
    grad_w, grad_b, grad_out = unpack(me, low, high)
    return grad_shard[None], grad_w, grad_b.reshape(HIDDEN), grad_out.reshape(HIDDEN)


def solution(mesh):
    split = Mesh(mesh.devices.reshape((2,) * 10), (*COLUMN, *DP))
    return jax.shard_map(
        shards,
        mesh=split,
        in_specs=(
            P(None, COLUMN, None),
            P(COLUMN, DP, None, None, None),
            P(COLUMN, DP, None, None),
            P(COLUMN, DP, None, None),
            P(COLUMN, DP, None, None),
            P((*COLUMN, *DP)),
            P(),
            P(),
            P(),
        ),
        out_specs=(P(DP, None, COLUMN, None), P(), P(), P()),
        check_vma=False,
    )
```
